256 devices in a mesh: row: 8 (over y, x_hi), col: 32 (over x_lo, z, core).
Axes of the slice: x: 4 (x_hi: 2, x_lo: 2; x = x_hi * 2 + x_lo), y: 4, z: 8, core: 2. Of those that a mesh axis runs over, the one named last changes fastest.
Arguments:
- spectra: bfloat16 [512, 2, 128, 4096], P('col', None, None, 'row'), may hold values from -150 to 150
- kept_bins: int32 [24], replicated, may hold values from 0 to 127, as said below
- keep_mask: int32 [512], P('col'), may hold values 0 or 1
Outputs:
- stack: bfloat16 [24, 2, 4096, 4096], P(None, None, 'row', 'col')
The draws below stay inside these ranges and needn't reach their ends.
Inputs may be any that keep to these rules, and one draw needn't show every extreme that they name: `kept_bins`: 24 distinct bins.
All inputs are finite; a program needn't handle non-finite values. No bound on the sum of `keep_mask` on one device may be relied on, other than what follows from the above.
Results may differ from the reference program's by a relative error of at most 0.0057.
Values may be sent and summed in bfloat16 or wider, within the bound.
A program may use at most 192 MiB of HBM per device.

```python
import math
import jax
import jax.numpy as jnp
from jax import lax

BINS = 24
BAND = 128
CHANNELS = 4096
WINDOWS = 512


def draw_spectra(key, part):
    key = jax.random.fold_in(key, 11)
    key_bins, key_cells, key_base = jax.random.split(key, 3)
    bin_scale = jnp.exp(jax.random.uniform(key_bins, (BAND,), jnp.float32, 0.0, math.log(10.0)))
    cell_scale = jnp.exp(jax.random.uniform(key_cells, (WINDOWS, 1, 1, CHANNELS), jnp.float32, math.log(0.3), math.log(3.0)))
    shape = (WINDOWS, 2, BAND, CHANNELS)
    base = jnp.clip(jax.random.normal(key_base, shape, jnp.float32), -5.0, 5.0)
    return (base * bin_scale[None, None, :, None] * cell_scale).astype(jnp.bfloat16)


def draw_kept_bins(key, part):
    key = jax.random.fold_in(key, 23)
    order = jax.random.permutation(key, BAND - 2).astype(jnp.int32) + 1
    ends = jnp.array([0, BAND - 1], dtype=jnp.int32)
    return jnp.concatenate([ends, order[:BINS - 2]]).astype(jnp.int32)


def plant(values, key, least, top_value):
    longest = values.shape.index(max(values.shape))
    spots = []
    for shift in (0, 1):
        where = [jax.random.randint(jax.random.fold_in(key, axis), (), 0, length) for axis, length in enumerate(values.shape)]
        where[longest] = (where[longest] + shift) % values.shape[longest]
        spots.append(tuple(where))
    return values.at[spots[0]].set(least).at[spots[1]].set(top_value)


def setup_inputs(seed: int = 0) -> dict:
    key_list = jax.random.split(jax.random.key(seed), 4)
    spectra = draw_spectra(jax.random.fold_in(key_list[3], 71), 0)
    kept_bins = draw_kept_bins(jax.random.fold_in(key_list[3], 71), 0)
    keep_mask = plant((jax.random.randint(key_list[2], (WINDOWS,), 0, 4) < 3).astype(jnp.int32), jax.random.fold_in(key_list[2], 1), 0, 1)
    return {"spectra": spectra, "kept_bins": kept_bins, "keep_mask": keep_mask}


def whiten(spectra, kept_bins, keep_mask):
    raw = spectra.astype(jnp.float32)
    power = lax.optimization_barrier(jnp.mean(raw * raw, axis=(1, 2)))
    factor = keep_mask.astype(jnp.float32)[:, None] / jnp.sqrt(power + 1e-06)
    band = spectra.shape[2]
    onehot = (kept_bins[:, None] == jnp.arange(band, dtype=jnp.int32)[None, :]).astype(jnp.float32)
    picked = jnp.einsum('fb,wpbc->fpwc', onehot, raw)
    return (picked * factor[None, None]).astype(jnp.bfloat16)

def reference(spectra, kept_bins, keep_mask):
    white = whiten(spectra, kept_bins, keep_mask)
    windows = spectra.shape[0]
    factor = 1.0 / math.sqrt(windows)

    def one_bin(pair):
        real_part, imag_part = pair
        left = jnp.concatenate([real_part, imag_part], 0)
        turned = jnp.concatenate([imag_part, -real_part], 0)
        dims = (((0,), (0,)), ((), ()))
        real_out = lax.dot_general(left, left, dims, preferred_element_type=jnp.float32)
        imag_out = lax.dot_general(turned, left, dims, preferred_element_type=jnp.float32)
        return (jnp.stack([real_out, imag_out], 0) * factor).astype(jnp.bfloat16)
    return lax.map(one_bin, (white[:, 0], white[:, 1]))
```

```python
import functools
import math

import jax
import jax.numpy as jnp
from jax import lax
from jax.experimental import pallas as pl
from jax.experimental.pallas import tpu as pltpu
from jax.sharding import PartitionSpec as P

MESH = pl.DeviceIdType.MESH
NX, NY, NZ = 4, 4, 8
BPC = 6
CB = 128


def whiten_kernel(bins_ref, mask_ref, s_ref, o_ref, tmp):
    windows, parts, band, width = s_ref.shape
    nb = bins_ref.shape[0]
    rows = lax.broadcasted_iota(jnp.int32, (parts * nb, parts * band), 0)
    cols = lax.broadcasted_iota(jnp.int32, (parts * nb, parts * band), 1)
    hot = jnp.zeros((parts * nb, parts * band), jnp.float32)
    for f in range(nb):
        for p in range(parts):
            hit = (rows == p * nb + f) & (cols == p * band + bins_ref[f])
            hot = jnp.where(hit, 1.0, hot)
    hot = hot.astype(jnp.bfloat16)
    for w in range(windows):
        block = s_ref[w].reshape(parts * band, width)
        raw = block.astype(jnp.float32)
        power = jnp.sum(raw * raw, axis=0, keepdims=True) * (1.0 / (parts * band))
        factor = mask_ref[w].astype(jnp.float32) / jnp.sqrt(power + 1e-06)
        picked = jnp.dot(hot, block, preferred_element_type=jnp.float32) * factor
        tmp[pl.ds(w, parts * nb, stride=windows), :] = picked
    white = tmp[...].reshape(parts, nb, windows, width).astype(jnp.bfloat16)
    for p in range(parts):
        o_ref[:, p] = white[p]


def whiten(spectra, kept_bins, keep_mask):
    windows, parts, band, width = spectra.shape
    nb = kept_bins.shape[0]
    lanes = 128
    return pl.pallas_call(
        whiten_kernel,
        grid=(width // lanes,),
        out_shape=jax.ShapeDtypeStruct((nb, parts, windows, width), jnp.bfloat16),
        in_specs=[
            pl.BlockSpec(memory_space=pltpu.SMEM),
            pl.BlockSpec(memory_space=pltpu.SMEM),
            pl.BlockSpec((windows, parts, band, lanes), lambda i: (0, 0, 0, i)),
        ],
        out_specs=pl.BlockSpec((nb, parts, windows, lanes), lambda i: (0, 0, 0, i)),
        scratch_shapes=[pltpu.VMEM((parts * nb * windows, lanes), jnp.float32)],
        compiler_params=pltpu.CompilerParams(vmem_limit_bytes=32 * 2**20),
        name="whiten",
    )(kept_bins, keep_mask, spectra)


def stack_kernel(
    white, out, R, C, O,
    s1_send, s1_recv, zp_send, zp_recv, zm_send, zm_recv,
    c_send, c_recv, b_send, b_recv, o_send, o_recv,
):
    row, col = lax.axis_index("row"), lax.axis_index("col")
    y, xh = row // 2, row % 2
    xl, z, c = col // 16, (col // 2) % 8, col % 2
    x = xh * 2 + xl
    slot = xl * 2 + c

    def at(x_, y_, z_, c_):
        return ((y_ % NY) * 2 + x_ // 2, (x_ % 2) * 16 + (z_ % NZ) * 2 + c_)

    primary = c == (z % 4) // 2
    source = primary & (y % 2 == z // 4)
    xd_own = y // 2
    ch_off = pl.multiple_of((z % 2) * 2 * CB, 2 * CB)

    barrier = pltpu.get_barrier_semaphore()
    others = [at((x + dx) % NX, y, z, (c + dc) % 2) for dx in range(NX) for dc in range(2) if dx or dc]
    others += [at(x, y, z + 1, c), at(x, y, z + NZ - 1, c)]
    others += [at(x, y + d, z, c) for d in (1, 2, 3)]
    for who in others:
        pl.semaphore_signal(barrier, inc=1, device_id=who, device_id_type=MESH)
    pl.semaphore_wait(barrier, len(others))

    def remote(src, dst, ssem, rsem, who):
        return pltpu.make_async_remote_copy(
            src_ref=src, dst_ref=dst, send_sem=ssem, recv_sem=rsem, device_id=who, device_id_type=MESH
        )

    def s1_copy(j, xt):
        return remote(
            white.at[xt, j], R.at[j, :, 0, pl.ds(pl.multiple_of(slot * 16, 16), 16), :],
            s1_send.at[j, xt], s1_recv.at[j, slot], at(xt, y, z, xh),
        )

    def s1_start(j):
        for d in range(NX):
            xt = (x + d) % NX
            self_ = (xt == x) & (xh == c)

            @pl.when(self_)
            def _():
                pltpu.make_async_copy(
                    white.at[xt, j], R.at[j, :, 0, pl.ds(pl.multiple_of(slot * 16, 16), 16), :],
                    s1_recv.at[j, slot],
                ).start()

            @pl.when(jnp.logical_not(self_))
            def _():
                s1_copy(j, xt).start()

    def s1_wait(j):
        for s in range(4):
            dst = R.at[j, :, 0, pl.ds(s * 16, 16), :]
            pltpu.make_async_copy(dst, dst, s1_recv.at[j, s]).wait()

    def zp_copy(j, t):
        who = at(x, y, z + 1, c)
        if t == 3:
            src, dst = R.at[j, 0, 5], R.at[j, 0, 7]
        else:
            src, dst = R.at[j, :, max(2 * t - 1, 0)], R.at[j, :, 2 * t + 1]
        return remote(src, dst, zp_send.at[j, t], zp_recv.at[j, t], who)

    def zm_copy(j, t):
        who = at(x, y, z + NZ - 1, c)
        if t == 3:
            src, dst = R.at[j, 1, 6], R.at[j, 1, 7]
        else:
            src, dst = R.at[j, :, 2 * t], R.at[j, :, 2 * t + 2]
        return remote(src, dst, zm_send.at[j, t], zm_recv.at[j, t], who)

    def span(t):
        return pl.ds(0, 1) if t == 0 else pl.ds(7, 1) if t == 4 else pl.ds(2 * t - 1, 2)

    def c_views(j, t, xd):
        src = R.at[j, :, span(t), :, pl.ds(ch_off, 2 * CB)]
        dst = C.at[j, :, span(t), :, pl.ds(pl.multiple_of(xd * 2 * CB, 2 * CB), 2 * CB)]
        return src, dst

    def c_copy(j, t, d):
        src, dst = c_views(j, t, xd_own)
        return remote(src, dst, c_send.at[j, t, d - 1], c_recv.at[j, t, xd_own], at(x, y + d, z, c))

    def c_start(j, t):
        @pl.when(source)
        def _():
            for d in (2, 1, 3):
                c_copy(j, t, d).start()
            src, dst = c_views(j, t, xd_own)
            pltpu.make_async_copy(src, dst, c_recv.at[j, t, xd_own]).start()

    def b_copy(j, t):
        view = C.at[j, :, span(t)]
        return remote(view, view, b_send.at[j, t], b_recv.at[j, t], at(x, y, z, 1 - c))

    def c_forward(j, t):
        @pl.when(primary)
        def _():
            for xd in range(2):
                _src, dst = c_views(j, t, xd)
                pltpu.make_async_copy(dst, dst, c_recv.at[j, t, xd]).wait()
            b_copy(j, t).start()

    def c_arrived(j):
        @pl.when(jnp.logical_not(primary))
        def _():
            for t in range(5):
                b_copy(j, t).wait_recv()

    def hop(j, t):
        if t == 0:
            s1_wait(j)
        else:
            zp_copy(j, t - 1).wait_recv()
            zm_copy(j, t - 1).wait_recv()
        if t < 4:
            zp_copy(j, t).start()
            zm_copy(j, t).start()
        c_start(j, t)

    scale = 1.0 / math.sqrt(512)
    dims = (((0,), (0,)), ((), ()))

    def product(j, xd):
        depth = R.shape[2] * R.shape[3]
        cols = pl.ds(xd * 2 * CB, 2 * CB)
        r0 = C[j, 0, :, :, cols].reshape(depth, 2 * CB)
        r1 = C[j, 1, :, :, cols].reshape(depth, 2 * CB)
        for m in range(2):
            rows = pl.ds(m * 256, 256)
            l0 = R[j, 0, :, :, rows].reshape(depth, 256)
            l1 = R[j, 1, :, :, rows].reshape(depth, 256)
            dot = functools.partial(lax.dot_general, dimension_numbers=dims, preferred_element_type=jnp.float32)
            re = ((dot(l0, r0) + dot(l1, r1)) * scale).astype(jnp.bfloat16)
            im = ((dot(l1, r0) - dot(l0, r1)) * scale).astype(jnp.bfloat16)
            for k in range(2):
                O[j, xd, k, 0, rows, :] = re[:, k * CB:(k + 1) * CB]
                O[j, xd, k, 1, rows, :] = im[:, k * CB:(k + 1) * CB]

    def o_copy(j, xd, k):
        return remote(
            O.at[j, xd, k], out.at[x, j], o_send.at[j, xd * 2 + k], o_recv.at[j, x], at(2 * c + xd, y, z, k)
        )

    def is_self(xd, k):
        return (2 * c + xd == x) & (k == c)

    def o_start(j, xd):
        for k in range(2):
            @pl.when(is_self(xd, k))
            def _():
                pltpu.make_async_copy(O.at[j, xd, k], out.at[x, j], o_recv.at[j, x]).start()

            @pl.when(jnp.logical_not(is_self(xd, k)))
            def _():
                o_copy(j, xd, k).start()

    def s1_all(j, carry):
        s1_start(j)
        return carry

    lax.fori_loop(0, BPC, s1_all, 0)

    def step(i, carry):
        def on(j, f):
            @pl.when((j >= 0) & (j < BPC))
            def _():
                f(j)

        def first(j):
            hop(j, 4)
            c_forward(j, 3)

        def second(j):
            hop(j, 2)
            c_forward(j, 1)

        on(i - 2, first)
        on(i - 1, second)
        on(i, lambda j: hop(j, 0))

        def third(j):
            c_forward(j, 4)
            c_arrived(j)
            product(j, 0)
            o_start(j, 0)

        on(i - 2, third)

        def fourth(j):
            hop(j, 3)
            c_forward(j, 2)

        on(i - 1, fourth)

        def fifth(j):
            hop(j, 1)
            c_forward(j, 0)

        on(i, fifth)

        def sixth(j):
            product(j, 1)
            o_start(j, 1)

        on(i - 2, sixth)
        return carry

    lax.fori_loop(0, BPC + 2, step, 0)

    def drain(j, carry):
        for xt in range(NX):
            @pl.when(jnp.logical_not((xt == x) & (xh == c)))
            def _():
                s1_copy(j, xt).wait_send()
        for t in range(4):
            zp_copy(j, t).wait_send()
            zm_copy(j, t).wait_send()

        @pl.when(source)
        def _():
            for t in range(5):
                for d in (1, 2, 3):
                    c_copy(j, t, d).wait_send()

        @pl.when(primary)
        def _():
            for t in range(5):
                b_copy(j, t).wait_send()
        for xd in range(2):
            for k in range(2):
                @pl.when(jnp.logical_not(is_self(xd, k)))
                def _():
                    o_copy(j, xd, k).wait_send()
        for xs in range(NX):
            dst = out.at[xs, j]
            pltpu.make_async_copy(dst, dst, o_recv.at[j, xs]).wait()
        return carry

    lax.fori_loop(0, BPC, drain, 0)


def stack(white):
    sems = [(BPC, 4)] * 6 + [(BPC, 5, 3), (BPC, 5, 2), (BPC, 5), (BPC, 5), (BPC, 4), (BPC, 4)]
    width = white.shape[-1]
    return pl.pallas_call(
        stack_kernel,
        out_shape=jax.ShapeDtypeStruct((NX, BPC, 2, width, CB), jnp.bfloat16),
        in_specs=[pl.BlockSpec(memory_space=pl.ANY)],
        out_specs=pl.BlockSpec(memory_space=pl.ANY),
        scratch_shapes=[
            pltpu.VMEM((BPC, 2, NZ, 64, width), jnp.bfloat16),
            pltpu.VMEM((BPC, 2, NZ, 64, 4 * CB), jnp.bfloat16),
            pltpu.VMEM((BPC, 2, 2, 2, width, CB), jnp.bfloat16),
        ] + [pltpu.SemaphoreType.DMA(s) for s in sems],
        compiler_params=pltpu.CompilerParams(
            collective_id=0, has_side_effects=True, vmem_limit_bytes=48 * 2**20
        ),
        cost_estimate=pl.CostEstimate(flops=6_442_450_944, bytes_accessed=16 * 2**20, transcendentals=0),
        name="stack",
    )(white)


def per_device(spectra, kept_bins, keep_mask):
    white = whiten(spectra, kept_bins, keep_mask)
    nb, parts, windows, width = white.shape
    tiles = stack(white.reshape(NX, BPC, parts, windows, width))
    return tiles.reshape(nb, parts, width, CB)


def solution(mesh):
    in_specs = (P("col", None, None, "row"), P(), P("col"))
    out_specs = P(None, None, "row", "col")
    return jax.shard_map(
        per_device, mesh=mesh, in_specs=in_specs, out_specs=out_specs, check_vma=False
    )
```

```python
import functools
import math

import jax
import jax.numpy as jnp
from jax import lax
from jax.experimental import pallas as pl
from jax.experimental.pallas import tpu as pltpu
from jax.sharding import PartitionSpec as P

MESH = pl.DeviceIdType.MESH
NX, NY, NZ = 4, 4, 8
BPC = 6
CB = 128
NH = 1


def stack_kernel(
    bins_ref, mask_ref, spectra, out, raw, picked, white, R, C, O,
    in_sem, s1_send, s1_recv, z_send, z_recv, c_send, c_recv, b_send, b_recv, o_send, o_recv,
):
    row, col = lax.axis_index("row"), lax.axis_index("col")
    y, xh = row // 2, row % 2
    xl, z, c = col // 16, (col // 2) % 8, col % 2
    x = xh * 2 + xl
    slot = xl * 2 + c

    def at(x_, y_, z_, c_):
        return ((y_ % NY) * 2 + x_ // 2, (x_ % 2) * 16 + (z_ % NZ) * 2 + c_)

    holder = (z % 4) // 2
    source = (c == holder) & (y % 2 == z // 4)
    to_core = y // 2
    ch_off = pl.multiple_of((z % 2) * 2 * CB, 2 * CB)
    y_from = 2 * c + z // 4

    barrier = pltpu.get_barrier_semaphore()

    def greet(who):
        pl.semaphore_signal(barrier, inc=1, device_id=who, device_id_type=MESH)

    ring = [at((x + dx) % NX, y, z, (c + dc) % 2) for dx in range(NX) for dc in range(2) if dx or dc]
    ring += [at(x, y, z + 1, c), at(x, y, z + NZ - 1, c)]
    for who in ring:
        greet(who)

    @pl.when(y_from != y)
    def _():
        greet(at(x, y_from, z, holder))

    windows, parts, band, width = raw.shape
    nb = bins_ref.shape[0]

    def in_copy(i):
        part = pl.ds(4 * i, 4)
        return pltpu.make_async_copy(spectra.at[part], raw.at[part], in_sem.at[i])

    for i in range(windows // 4):
        in_copy(i).start()
    rows = lax.broadcasted_iota(jnp.int32, (parts * nb, parts * band), 0)
    cols = lax.broadcasted_iota(jnp.int32, (parts * nb, parts * band), 1)
    place = jnp.full((parts * nb, parts * band), -1, jnp.int32)
    for f in range(nb):
        for p in range(parts):
            place = jnp.where(rows == p * nb + f, bins_ref[f] + p * band, place)
    hot = jnp.where(cols == place, 1.0, 0.0).astype(jnp.bfloat16)

    def whiten(i, carry):
        in_copy(i).wait()
        for k in range(4):
            w = 4 * i + k
            block = raw[w].reshape(parts * band, width)
            wide = block.astype(jnp.float32)
            power = jnp.sum(wide * wide, axis=0, keepdims=True) * (1.0 / (parts * band))
            factor = mask_ref[w].astype(jnp.float32) / jnp.sqrt(power + 1e-06)
            kept = jnp.dot(hot, block, preferred_element_type=jnp.float32) * factor
            for l in range(width // 128):
                picked[l, pl.ds(w, parts * nb, stride=windows), :] = kept[:, l * 128:(l + 1) * 128]
        return carry

    lax.fori_loop(0, windows // 4, whiten, 0)
    pl.semaphore_wait(barrier, len(ring) + jnp.where(source, NY - 1, 0))

    def remote(src, dst, ssem, rsem, who):
        return pltpu.make_async_remote_copy(
            src_ref=src, dst_ref=dst, send_sem=ssem, recv_sem=rsem, device_id=who, device_id_type=MESH
        )

    def s1_copy(j, xt):
        return remote(
            white.at[xt, j], R.at[xh, j, :, 0, pl.ds(pl.multiple_of(slot * 16, 16), 16), :],
            s1_send.at[xt], s1_recv.at[j], at(xt, y, z, xh),
        )

    def s1_start(j):
        for d in range(NX):
            xt = (x + d) % NX
            self_ = (xt == x) & (xh == c)

            @pl.when(self_)
            def _():
                pltpu.make_async_copy(
                    white.at[xt, j], R.at[xh, j, :, 0, pl.ds(pl.multiple_of(slot * 16, 16), 16), :],
                    s1_recv.at[j],
                ).start()

            @pl.when(jnp.logical_not(self_))
            def _():
                s1_copy(j, xt).start()

    def s1_wait(j):
        dst = R.at[c, j, :, 0]
        pltpu.make_async_copy(dst, dst, s1_recv.at[j]).wait()

    def z_copy(j, t, p, h, way):
        rows = pl.ds(h * (64 // NH), 64 // NH)
        if way == 0:
            here, there, who = max(2 * t - 1, 0), 2 * t + 1, at(x, y, z + 1, c)
        else:
            here, there, who = 2 * t, 7 if t == 3 else 2 * t + 2, at(x, y, z + NZ - 1, c)
        return remote(
            R.at[c, j, p, here, rows], R.at[c, j, p, there, rows],
            z_send.at[way], z_recv.at[j % 2, t, p, h, way], who,
        )

    def z_goes(t, p, way):
        return 0 <= t < 3 or (t == 3 and way == p)

    def span(t):
        return {1: pl.ds(0, 3), 2: pl.ds(3, 2), 3: pl.ds(5, 2), 4: pl.ds(7, 1)}[t]

    def b_copy(j, view):
        view = R.at[c, j, :, view]
        return remote(view, view, b_send, b_recv.at[j], at(x, y, z, 1 - c))

    def c_copy(j, view, d):
        src, dst = R.at[c, j, :, view, :, pl.ds(ch_off, 2 * CB)], C.at[j, :, view]
        return remote(src, dst, c_send.at[d], c_recv.at[j], at(x, y + d, z, to_core))

    def share(j, t):
        @pl.when(source)
        def _():
            for d in (2, 1, 3):
                c_copy(j, span(t), d).start()

            @pl.when(c == to_core)
            def _():
                pltpu.make_async_copy(
                    R.at[c, j, :, span(t), :, pl.ds(ch_off, 2 * CB)], C.at[j, :, span(t)], c_recv.at[j]
                ).start()

            @pl.when(c != to_core)
            def _():
                c_copy(j, span(t), 0).start()

        b_copy(j, span(t)).start()

    def shared(j):
        dst = R.at[1 - c, j]
        pltpu.make_async_copy(dst, dst, b_recv.at[j]).wait()
        pltpu.make_async_copy(C.at[j], C.at[j], c_recv.at[j]).wait()

    def hop(j, t):
        if t == 0:
            s1_wait(j)
        for p in range(parts):
            for h in range(NH):
                for way in range(2):
                    if z_goes(t - 1, p, way):
                        z_copy(j, t - 1, p, h, way).wait_recv()
                    if z_goes(t, p, way):
                        z_copy(j, t, p, h, way).start()
        if t > 0:
            share(j, t)

    scale = 1.0 / math.sqrt(512)
    dims = (((0,), (0,)), ((), ()))

    def product(j, xr, m):
        depth = R.shape[3] * R.shape[4]
        rows = pl.ds(m * 256, 256)
        r0, r1 = (C[j, p].reshape(depth, 2 * CB) for p in range(parts))
        l0, l1 = (R[xr, j, p, :, :, rows].reshape(depth, 256) for p in range(parts))
        dot = functools.partial(lax.dot_general, dimension_numbers=dims, preferred_element_type=jnp.float32)
        re = ((dot(l0, r0) + dot(l1, r1)) * scale).astype(jnp.bfloat16)
        im = ((dot(l1, r0) - dot(l0, r1)) * scale).astype(jnp.bfloat16)
        for k in range(2):
            O[j, xr, k, 0, rows, :] = re[:, k * CB:(k + 1) * CB]
            O[j, xr, k, 1, rows, :] = im[:, k * CB:(k + 1) * CB]
        o_start(j, xr, m)

    def o_copy(j, xr, k, m):
        rows = pl.ds(m * 256, 256)
        return remote(
            O.at[j, xr, k, :, rows], out.at[x, j, :, rows],
            o_send.at[xr * 2 + k], o_recv, at(2 * xr + c, y, z, k)
        )

    def is_self(xr, k):
        return (2 * xr + c == x) & (k == c)

    def o_start(j, xr, m):
        rows = pl.ds(m * 256, 256)
        for k in range(2):
            @pl.when(is_self(xr, k))
            def _():
                pltpu.make_async_copy(
                    O.at[j, xr, k, :, rows], out.at[x, j, :, rows], o_recv
                ).start()

            @pl.when(jnp.logical_not(is_self(xr, k)))
            def _():
                o_copy(j, xr, k, m).start()

    def s1_bin(j):
        for l in range(width // 128):
            for xt in range(NX):
                for p in range(parts):
                    start = pl.multiple_of((p * nb + xt * BPC + j) * windows, windows)
                    tile = picked[l, pl.ds(start, windows), :]
                    white[xt, j, p, :, l * 128:(l + 1) * 128] = tile.astype(jnp.bfloat16)
        s1_start(j)

    s1_bin(0)
    hop(0, 0)
    s1_bin(1)
    hop(0, 1)
    s1_bin(2)
    hop(0, 2)
    hop(1, 0)

    def step(i, carry):
        def on(j, *work):
            @pl.when((j >= 0) & (j < BPC))
            def _():
                for f, *args in work:
                    f(j, *args)

        on(i, (hop, 3))
        on(i - 1, (product, 0, 1))
        on(i + 1, (hop, 1))
        on(i - 1, (product, 1, 0))
        on(i, (hop, 4))
        on(i - 1, (product, 1, 1))
        on(i + 2, (hop, 0))
        on(i + 1, (hop, 2))
        on(i + 3, (s1_bin,))
        on(i, (shared,), (product, 0, 0))
        return carry

    lax.fori_loop(0, BPC + 1, step, 0)

    def sent(view, sem):
        remote(view, view, sem, o_recv, at(x, y, z, 1 - c)).wait_send()

    for xt in range(NX):
        @pl.when(jnp.logical_not((xt == x) & (xh == c)))
        def _():
            sent(white.at[xt], s1_send.at[xt])
    for way in range(2):
        sent(R.at[c, :, 0, pl.ds(0, 7)], z_send.at[way])
    sent(R.at[c], b_send)

    @pl.when(source)
    def _():
        for d in range(1, 4):
            sent(C, c_send.at[d])

        @pl.when(c != to_core)
        def _():
            sent(C, c_send.at[0])

    for xr in range(2):
        for k in range(2):
            @pl.when(jnp.logical_not(is_self(xr, k)))
            def _():
                sent(O.at[:, xr, k], o_send.at[xr * 2 + k])
    pltpu.make_async_copy(out, out, o_recv).wait()


def per_device(spectra, kept_bins, keep_mask):
    windows, parts, band, width = spectra.shape
    nb = kept_bins.shape[0]
    sems = [(windows // 4,), (NX,), (BPC,), (2,), (2, 4, 2, NH, 2), (NY,), (BPC,), (), (BPC,), (4,), ()]
    tiles = pl.pallas_call(
        stack_kernel,
        out_shape=pltpu.VMEM((NX, BPC, parts, width, CB), jnp.bfloat16),
        in_specs=[
            pl.BlockSpec(memory_space=pltpu.SMEM),
            pl.BlockSpec(memory_space=pltpu.SMEM),
            pl.BlockSpec(memory_space=pltpu.HBM),
        ],
        out_specs=pl.BlockSpec(memory_space=pl.ANY),
        scratch_shapes=[
            pltpu.VMEM((windows, parts, band, width), jnp.bfloat16),
            pltpu.VMEM((width // 128, parts * nb * windows, 128), jnp.float32),
            pltpu.VMEM((NX, BPC, parts, windows, width), jnp.bfloat16),
            pltpu.VMEM((2, BPC, parts, NZ, 4 * windows, width), jnp.bfloat16),
            pltpu.VMEM((BPC, parts, NZ, 4 * windows, 2 * CB), jnp.bfloat16),
            pltpu.VMEM((BPC, 2, 2, parts, width, CB), jnp.bfloat16),
        ] + [pltpu.SemaphoreType.DMA(s) for s in sems],
        compiler_params=pltpu.CompilerParams(
            collective_id=0, has_side_effects=True, vmem_limit_bytes=54 * 2**20
        ),
        cost_estimate=pl.CostEstimate(flops=6_442_450_944, bytes_accessed=16 * 2**20, transcendentals=0),
        name="stack",
    )(kept_bins, keep_mask, spectra)
    return tiles.reshape(nb, parts, width, CB)


def solution(mesh):
    in_specs = (P("col", None, None, "row"), P(), P("col"))
    out_specs = P(None, None, "row", "col")
    return jax.shard_map(
        per_device, mesh=mesh, in_specs=in_specs, out_specs=out_specs, check_vma=False
    )
```

```python
import functools
import math

import jax
import jax.numpy as jnp
from jax import lax
from jax.experimental import pallas as pl
from jax.experimental.pallas import tpu as pltpu
from jax.sharding import PartitionSpec as P

MESH = pl.DeviceIdType.MESH
NX, NY, NZ = 4, 4, 8
BPC = 6
CB = 128
NH = 2


def stack_kernel(
    bins_ref, mask_ref, spectra, out, raw, picked, white, R, C, O,
    in_sem, s1_send, s1_recv, z_send, z_recv, c_send, c_recv, b_send, b_recv, o_send, o_recv,
):
    row, col = lax.axis_index("row"), lax.axis_index("col")
    y, xh = row // 2, row % 2
    xl, z, c = col // 16, (col // 2) % 8, col % 2
    x = xh * 2 + xl
    slot = xl * 2 + c

    def at(x_, y_, z_, c_):
        return ((y_ % NY) * 2 + x_ // 2, (x_ % 2) * 16 + (z_ % NZ) * 2 + c_)

    holder = (z % 4) // 2
    source = (c == holder) & (y % 2 == z // 4)
    to_core = y // 2
    y_from = 2 * c + z // 4

    barrier = pltpu.get_barrier_semaphore()

    def greet(who):
        pl.semaphore_signal(barrier, inc=1, device_id=who, device_id_type=MESH)

    ring = [at((x + dx) % NX, y, z, (c + dc) % 2) for dx in range(NX) for dc in range(2) if dx or dc]
    ring += [at(x, y, z + 1, c), at(x, y, z + NZ - 1, c)]
    for who in ring:
        greet(who)

    @pl.when(y_from != y)
    def _():
        greet(at(x, y_from, z, holder))

    windows, parts, band, width = raw.shape
    nb = bins_ref.shape[0]

    def in_copy(i):
        part = pl.ds(4 * i, 4)
        return pltpu.make_async_copy(spectra.at[part], raw.at[part], in_sem.at[i])

    for i in range(windows // 4):
        in_copy(i).start()
    rows = lax.broadcasted_iota(jnp.int32, (parts * nb, parts * band), 0)
    cols = lax.broadcasted_iota(jnp.int32, (parts * nb, parts * band), 1)
    place = jnp.full((parts * nb, parts * band), -1, jnp.int32)
    for f in range(nb):
        for p in range(parts):
            place = jnp.where(rows == p * nb + f, bins_ref[f] + p * band, place)
    hot = jnp.where(cols == place, 1.0, 0.0).astype(jnp.bfloat16)

    def whiten(i, carry):
        in_copy(i).wait()
        for k in range(4):
            w = 4 * i + k
            block = raw[w].reshape(parts * band, width)
            wide = block.astype(jnp.float32)
            power = jnp.sum(wide * wide, axis=0, keepdims=True) * (1.0 / (parts * band))
            factor = mask_ref[w].astype(jnp.float32) / jnp.sqrt(power + 1e-06)
            kept = jnp.dot(hot, block, preferred_element_type=jnp.float32) * factor
            for l in range(width // 128):
                picked[l, pl.ds(w, parts * nb, stride=windows), :] = kept[:, l * 128:(l + 1) * 128]
        return carry

    lax.fori_loop(0, windows // 4, whiten, 0)
    pl.semaphore_wait(barrier, len(ring) + jnp.where(source, NY - 1, 0))

    def remote(src, dst, ssem, rsem, who):
        return pltpu.make_async_remote_copy(
            src_ref=src, dst_ref=dst, send_sem=ssem, recv_sem=rsem, device_id=who, device_id_type=MESH
        )

    def s1_copy(j, xt):
        return remote(
            white.at[xt, j], R.at[xh, j, :, 0, :, pl.ds(pl.multiple_of(slot * 16, 16), 16), :],
            s1_send.at[xt], s1_recv.at[j, xl], at(xt, y, z, xh),
        )

    def s1_start(j):
        for d in range(NX):
            xt = (x + d) % NX
            self_ = (xt == x) & (xh == c)

            @pl.when(self_)
            def _():
                pltpu.make_async_copy(
                    white.at[xt, j], R.at[xh, j, :, 0, :, pl.ds(pl.multiple_of(slot * 16, 16), 16), :],
                    s1_recv.at[j, xl],
                ).start()

            @pl.when(jnp.logical_not(self_))
            def _():
                s1_copy(j, xt).start()

    def s1_wait(j, h):
        dst = R.at[c, j, :, 0, :, pl.ds(h * 32, 32)]
        pltpu.make_async_copy(dst, dst, s1_recv.at[j, h]).wait()

    def z_copy(j, t, p, h, way):
        rows = pl.ds(h * (64 // NH), 64 // NH)
        if way == 0:
            here, there, who = max(2 * t - 1, 0), 2 * t + 1, at(x, y, z + 1, c)
        else:
            here, there, who = 2 * t, 7 if t == 3 else 2 * t + 2, at(x, y, z + NZ - 1, c)
        return remote(
            R.at[c, j, p, here, :, rows], R.at[c, j, p, there, :, rows],
            z_send.at[way], z_recv.at[j % 2, t, p, h, way], who,
        )

    def z_goes(t, p, way):
        return 0 <= t < 3 or (t == 3 and way == p)

    def span(t):
        return {1: pl.ds(0, 3), 2: pl.ds(3, 2), 3: pl.ds(5, 2), 4: pl.ds(7, 1)}[t]

    def b_copy(j, view):
        view = R.at[c, j, :, view]
        return remote(view, view, b_send, b_recv.at[j], at(x, y, z, 1 - c))

    def c_copy(j, view, d):
        src, dst = R.at[c, j, :, view, z % 2], C.at[j, :, view]
        return remote(src, dst, c_send.at[d], c_recv.at[j], at(x, y + d, z, to_core))

    def share(j, t):
        @pl.when(source)
        def _():
            for d in (2, 1, 3):
                c_copy(j, span(t), d).start()

            @pl.when(c == to_core)
            def _():
                pltpu.make_async_copy(
                    R.at[c, j, :, span(t), z % 2], C.at[j, :, span(t)], c_recv.at[j]
                ).start()

            @pl.when(c != to_core)
            def _():
                c_copy(j, span(t), 0).start()

        b_copy(j, span(t)).start()

    def shared(j):
        dst = R.at[1 - c, j]
        pltpu.make_async_copy(dst, dst, b_recv.at[j]).wait()
        pltpu.make_async_copy(C.at[j], C.at[j], c_recv.at[j]).wait()

    def hop(j, t):
        for h in range(NH):
            if t == 0:
                s1_wait(j, h)
            for p in range(parts):
                for way in range(2):
                    if z_goes(t - 1, p, way):
                        z_copy(j, t - 1, p, h, way).wait_recv()
                    if z_goes(t, p, way):
                        z_copy(j, t, p, h, way).start()
        if t > 0:
            share(j, t)

    scale = 1.0 / math.sqrt(512)
    dims = (((0,), (0,)), ((), ()))

    def product(j, xr, m):
        depth = R.shape[3] * R.shape[5]
        rows = pl.ds(m * 256, 256)
        r0, r1 = (C[j, p].reshape(depth, 2 * CB) for p in range(parts))
        l0, l1 = (R[xr, j, p, :, m].reshape(depth, 256) for p in range(parts))
        dot = functools.partial(lax.dot_general, dimension_numbers=dims, preferred_element_type=jnp.float32)
        re = ((dot(l0, r0) + dot(l1, r1)) * scale).astype(jnp.bfloat16)
        im = ((dot(l1, r0) - dot(l0, r1)) * scale).astype(jnp.bfloat16)
        for k in range(2):
            O[j, xr, k, 0, rows, :] = re[:, k * CB:(k + 1) * CB]
            O[j, xr, k, 1, rows, :] = im[:, k * CB:(k + 1) * CB]
        o_start(j, xr, m)

    def o_copy(j, xr, k, m):
        rows = pl.ds(m * 256, 256)
        return remote(
            O.at[j, xr, k, :, rows], out.at[x, j, :, rows],
            o_send.at[xr * 2 + k], o_recv, at(2 * xr + c, y, z, k)
        )

    def is_self(xr, k):
        return (2 * xr + c == x) & (k == c)

    def o_start(j, xr, m):
        rows = pl.ds(m * 256, 256)
        for k in range(2):
            @pl.when(is_self(xr, k))
            def _():
                pltpu.make_async_copy(
                    O.at[j, xr, k, :, rows], out.at[x, j, :, rows], o_recv
                ).start()

            @pl.when(jnp.logical_not(is_self(xr, k)))
            def _():
                o_copy(j, xr, k, m).start()

    def s1_bin(j):
        for l in range(width // 128):
            for xt in range(NX):
                for p in range(parts):
                    start = pl.multiple_of((p * nb + xt * BPC + j) * windows, windows)
                    tile = picked[l, pl.ds(start, windows), :]
                    white[xt, j, p, l // 2, :, l % 2 * 128:(l % 2 + 1) * 128] = tile.astype(jnp.bfloat16)
        s1_start(j)

    s1_bin(0)
    hop(0, 0)
    s1_bin(1)
    s1_bin(2)
    hop(0, 1)
    s1_bin(3)
    s1_bin(4)
    s1_bin(5)
    hop(0, 2)
    hop(1, 0)

    def step(i, carry):
        def on(j, *work):
            @pl.when((j >= 0) & (j < BPC))
            def _():
                for f, *args in work:
                    f(j, *args)

        on(i, (hop, 3))
        on(i - 1, (product, 0, 1))
        on(i + 1, (hop, 1))
        on(i - 1, (product, 1, 0))
        on(i, (hop, 4))
        on(i - 1, (product, 1, 1))
        on(i + 2, (hop, 0))
        on(i + 1, (hop, 2))
        on(i, (shared,), (product, 0, 0))
        return carry

    lax.fori_loop(0, BPC + 1, step, 0)

    def sent(view, sem):
        remote(view, view, sem, o_recv, at(x, y, z, 1 - c)).wait_send()

    for xt in range(NX):
        @pl.when(jnp.logical_not((xt == x) & (xh == c)))
        def _():
            sent(white.at[xt], s1_send.at[xt])
    for way in range(2):
        sent(R.at[c, :, 0, pl.ds(0, 7)], z_send.at[way])
    sent(R.at[c], b_send)

    @pl.when(source)
    def _():
        for d in range(1, 4):
            sent(C, c_send.at[d])

        @pl.when(c != to_core)
        def _():
            sent(C, c_send.at[0])

    for xr in range(2):
        for k in range(2):
            @pl.when(jnp.logical_not(is_self(xr, k)))
            def _():
                sent(O.at[:, xr, k], o_send.at[xr * 2 + k])
    pltpu.make_async_copy(out, out, o_recv).wait()


def per_device(spectra, kept_bins, keep_mask):
    windows, parts, band, width = spectra.shape
    nb = kept_bins.shape[0]
    sems = [(windows // 4,), (NX,), (BPC, NH), (2,), (2, 4, 2, NH, 2), (NY,), (BPC,), (), (BPC,), (4,), ()]
    tiles = pl.pallas_call(
        stack_kernel,
        out_shape=pltpu.VMEM((NX, BPC, parts, width, CB), jnp.bfloat16),
        in_specs=[
            pl.BlockSpec(memory_space=pltpu.SMEM),
            pl.BlockSpec(memory_space=pltpu.SMEM),
            pl.BlockSpec(memory_space=pltpu.HBM),
        ],
        out_specs=pl.BlockSpec(memory_space=pl.ANY),
        scratch_shapes=[
            pltpu.VMEM((windows, parts, band, width), jnp.bfloat16),
            pltpu.VMEM((width // 128, parts * nb * windows, 128), jnp.float32),
            pltpu.VMEM((NX, BPC, parts, 2, windows, 2 * CB), jnp.bfloat16),
            pltpu.VMEM((2, BPC, parts, NZ, 2, 4 * windows, 2 * CB), jnp.bfloat16),
            pltpu.VMEM((BPC, parts, NZ, 4 * windows, 2 * CB), jnp.bfloat16),
            pltpu.VMEM((BPC, 2, 2, parts, width, CB), jnp.bfloat16),
        ] + [pltpu.SemaphoreType.DMA(s) for s in sems],
        compiler_params=pltpu.CompilerParams(
            collective_id=0, has_side_effects=True, vmem_limit_bytes=54 * 2**20
        ),
        cost_estimate=pl.CostEstimate(flops=6_442_450_944, bytes_accessed=16 * 2**20, transcendentals=0),
        name="stack",
    )(kept_bins, keep_mask, spectra)
    return tiles.reshape(nb, parts, width, CB)


def solution(mesh):
    in_specs = (P("col", None, None, "row"), P(), P("col"))
    out_specs = P(None, None, "row", "col")
    return jax.shard_map(
        per_device, mesh=mesh, in_specs=in_specs, out_specs=out_specs, check_vma=False
    )
```

```python
import functools
import math

import jax
import jax.numpy as jnp
from jax import lax
from jax.experimental import pallas as pl
from jax.experimental.pallas import tpu as pltpu
from jax.sharding import PartitionSpec as P

MESH = pl.DeviceIdType.MESH
NX, NY, NZ = 4, 4, 8
BPC = 6
CB = 128
NH = 2


def stack_kernel(
    bins_ref, mask_ref, spectra, out, raw, picked, white, R, C, O,
    in_sem, s1_send, s1_recv, z_send, z_recv, c_send, c_recv, b_send, b_recv, o_send, o_recv,
):
    row, col = lax.axis_index("row"), lax.axis_index("col")
    y, xh = row // 2, row % 2
    xl, z, c = col // 16, (col // 2) % 8, col % 2
    x = xh * 2 + xl
    slot = xl * 2 + c

    def at(x_, y_, z_, c_):
        return ((y_ % NY) * 2 + x_ // 2, (x_ % 2) * 16 + (z_ % NZ) * 2 + c_)

    holder = (z % 4) // 2
    source = (c == holder) & (y % 2 == z // 4)
    to_core = y // 2
    y_from = 2 * c + z // 4

    barrier = pltpu.get_barrier_semaphore()

    def greet(who):
        pl.semaphore_signal(barrier, inc=1, device_id=who, device_id_type=MESH)

    ring = [at((x + dx) % NX, y, z, (c + dc) % 2) for dx in range(NX) for dc in range(2) if dx or dc]
    ring += [at(x, y, z + 1, c), at(x, y, z + NZ - 1, c)]
    for who in ring:
        greet(who)

    @pl.when(y_from != y)
    def _():
        greet(at(x, y_from, z, holder))

    windows, parts, band, width = raw.shape
    nb = bins_ref.shape[0]

    def in_copy(i):
        part = pl.ds(4 * i, 4)
        return pltpu.make_async_copy(spectra.at[part], raw.at[part], in_sem.at[i])

    for i in range(windows // 4):
        in_copy(i).start()
    rows = lax.broadcasted_iota(jnp.int32, (parts * nb, parts * band), 0)
    cols = lax.broadcasted_iota(jnp.int32, (parts * nb, parts * band), 1)
    place = jnp.full((parts * nb, parts * band), -1, jnp.int32)
    for f in range(nb):
        for p in range(parts):
            place = jnp.where(rows == p * nb + f, bins_ref[f] + p * band, place)
    hot = jnp.where(cols == place, 1.0, 0.0).astype(jnp.bfloat16)

    def whiten(i, carry):
        in_copy(i).wait()
        for k in range(4):
            w = 4 * i + k
            block = raw[w].reshape(parts * band, width)
            wide = block.astype(jnp.float32)
            power = jnp.sum(wide * wide, axis=0, keepdims=True) * (1.0 / (parts * band))
            factor = mask_ref[w].astype(jnp.float32) / jnp.sqrt(power + 1e-06)
            kept = jnp.dot(hot, block, preferred_element_type=jnp.float32) * factor
            for l in range(width // 128):
                picked[l, pl.ds(w, parts * nb, stride=windows), :] = kept[:, l * 128:(l + 1) * 128]
        return carry

    lax.fori_loop(0, windows // 4, whiten, 0)
    pl.semaphore_wait(barrier, len(ring) + jnp.where(source, NY - 1, 0))

    def remote(src, dst, ssem, rsem, who):
        return pltpu.make_async_remote_copy(
            src_ref=src, dst_ref=dst, send_sem=ssem, recv_sem=rsem, device_id=who, device_id_type=MESH
        )

    def s1_copy(j, xt):
        return remote(
            white.at[xt, j], R.at[xh, j, :, 0, :, pl.ds(pl.multiple_of(slot * 16, 16), 16), :],
            s1_send.at[xt], s1_recv.at[j, xl], at(xt, y, z, xh),
        )

    def s1_start(j):
        for d in range(NX):
            xt = (x + d) % NX
            self_ = (xt == x) & (xh == c)

            @pl.when(self_)
            def _():
                pltpu.make_async_copy(
                    white.at[xt, j], R.at[xh, j, :, 0, :, pl.ds(pl.multiple_of(slot * 16, 16), 16), :],
                    s1_recv.at[j, xl],
                ).start()

            @pl.when(jnp.logical_not(self_))
            def _():
                s1_copy(j, xt).start()

    def s1_wait(j, h):
        dst = R.at[c, j, :, 0, :, pl.ds(h * 32, 32)]
        pltpu.make_async_copy(dst, dst, s1_recv.at[j, h]).wait()

    def z_copy(j, t, p, h, way):
        rows = pl.ds(h * (64 // NH), 64 // NH)
        if way == 0:
            here, there, who = max(2 * t - 1, 0), 2 * t + 1, at(x, y, z + 1, c)
        else:
            here, there, who = 2 * t, 7 if t == 3 else 2 * t + 2, at(x, y, z + NZ - 1, c)
        return remote(
            R.at[c, j, p, here, :, rows], R.at[c, j, p, there, :, rows],
            z_send.at[way], z_recv.at[j % 2, t, p, h, way], who,
        )

    def z_goes(t, p, way):
        return 0 <= t < 3 or (t == 3 and way == p)

    def span(t):
        return pl.ds(0, 1) if t == 0 else pl.ds(7, 1) if t == 4 else pl.ds(2 * t - 1, 2)

    def b_copy(j, view):
        view = R.at[c, j, :, view]
        return remote(view, view, b_send, b_recv.at[j], at(x, y, z, 1 - c))

    def c_copy(j, view, d):
        src, dst = R.at[c, j, :, view, z % 2], C.at[j, :, view]
        return remote(src, dst, c_send.at[d], c_recv.at[j], at(x, y + d, z, to_core))

    def share(j, t):
        @pl.when(source)
        def _():
            for d in (2, 1, 3):
                c_copy(j, span(t), d).start()

            @pl.when(c == to_core)
            def _():
                pltpu.make_async_copy(
                    R.at[c, j, :, span(t), z % 2], C.at[j, :, span(t)], c_recv.at[j]
                ).start()

            @pl.when(c != to_core)
            def _():
                c_copy(j, span(t), 0).start()

        b_copy(j, span(t)).start()

    def shared(j):
        dst = R.at[1 - c, j]
        pltpu.make_async_copy(dst, dst, b_recv.at[j]).wait()
        pltpu.make_async_copy(C.at[j], C.at[j], c_recv.at[j]).wait()

    def hop(j, t):
        for h in range(NH):
            if t == 0:
                s1_wait(j, h)
            for p in range(parts):
                for way in range(2):
                    if z_goes(t - 1, p, way):
                        z_copy(j, t - 1, p, h, way).wait_recv()
                    if z_goes(t, p, way):
                        z_copy(j, t, p, h, way).start()
        share(j, t)

    scale = 1.0 / math.sqrt(512)
    dims = (((0,), (0,)), ((), ()))

    def product(j, turn, m):
        xr = jnp.where(turn == 0, 1 - x // 2, x // 2)
        depth = R.shape[3] * R.shape[5]
        rows = pl.ds(m * 256, 256)
        r0, r1 = (C[j, p].reshape(depth, 2 * CB) for p in range(parts))
        l0, l1 = (R[xr, j, p, :, m].reshape(depth, 256) for p in range(parts))
        both = jnp.concatenate([r0, r1], 1)
        dot = functools.partial(lax.dot_general, dimension_numbers=dims, preferred_element_type=jnp.float32)
        by0, by1 = dot(l0, both), dot(l1, both)
        re = ((by0[:, :2 * CB] + by1[:, 2 * CB:]) * scale).astype(jnp.bfloat16)
        im = ((by1[:, :2 * CB] - by0[:, 2 * CB:]) * scale).astype(jnp.bfloat16)
        for k in range(2):
            O[j, xr, k, 0, rows, :] = re[:, k * CB:(k + 1) * CB]
            O[j, xr, k, 1, rows, :] = im[:, k * CB:(k + 1) * CB]
        o_start(j, xr, m)

    def o_copy(j, xr, k, m):
        rows = pl.ds(m * 256, 256)
        return remote(
            O.at[j, xr, k, :, rows], out.at[x, j, :, rows],
            o_send.at[xr * 2 + k], o_recv, at(2 * xr + c, y, z, k)
        )

    def is_self(xr, k):
        return (2 * xr + c == x) & (k == c)

    def o_start(j, xr, m):
        rows = pl.ds(m * 256, 256)
        for k in range(2):
            @pl.when(is_self(xr, k))
            def _():
                pltpu.make_async_copy(
                    O.at[j, xr, k, :, rows], out.at[x, j, :, rows], o_recv
                ).start()

            @pl.when(jnp.logical_not(is_self(xr, k)))
            def _():
                o_copy(j, xr, k, m).start()

    def s1_bin(j):
        for l in range(width // 128):
            for xt in range(NX):
                for p in range(parts):
                    start = pl.multiple_of((p * nb + xt * BPC + j) * windows, windows)
                    tile = picked[l, pl.ds(start, windows), :]
                    white[xt, j, p, l // 2, :, l % 2 * 128:(l % 2 + 1) * 128] = tile.astype(jnp.bfloat16)
        s1_start(j)

    s1_bin(0)
    hop(0, 0)
    s1_bin(1)
    s1_bin(2)
    hop(0, 1)
    s1_bin(3)
    s1_bin(4)
    s1_bin(5)
    hop(0, 2)
    hop(1, 0)

    def step(i, carry):
        def on(j, *work):
            @pl.when((j >= 0) & (j < BPC))
            def _():
                for f, *args in work:
                    f(j, *args)

        on(i, (hop, 3))
        on(i - 1, (product, 0, 1))
        on(i + 1, (hop, 1))
        on(i - 1, (product, 1, 0))
        on(i, (hop, 4))
        on(i - 1, (product, 1, 1))
        on(i + 2, (hop, 0))
        on(i + 1, (hop, 2))
        on(i, (shared,), (product, 0, 0))
        return carry

    lax.fori_loop(0, BPC + 1, step, 0)

    def sent(view, sem):
        remote(view, view, sem, o_recv, at(x, y, z, 1 - c)).wait_send()

    for xt in range(NX):
        @pl.when(jnp.logical_not((xt == x) & (xh == c)))
        def _():
            sent(white.at[xt], s1_send.at[xt])
    for way in range(2):
        sent(R.at[c, :, 0, pl.ds(0, 7)], z_send.at[way])
    sent(R.at[c], b_send)

    @pl.when(source)
    def _():
        for d in range(1, 4):
            sent(C, c_send.at[d])

        @pl.when(c != to_core)
        def _():
            sent(C, c_send.at[0])

    for xr in range(2):
        for k in range(2):
            @pl.when(jnp.logical_not(is_self(xr, k)))
            def _():
                sent(O.at[:, xr, k], o_send.at[xr * 2 + k])
    pltpu.make_async_copy(out, out, o_recv).wait()


def per_device(spectra, kept_bins, keep_mask):
    windows, parts, band, width = spectra.shape
    nb = kept_bins.shape[0]
    sems = [(windows // 4,), (NX,), (BPC, NH), (2,), (2, 4, 2, NH, 2), (NY,), (BPC,), (), (BPC,), (4,), ()]
    tiles = pl.pallas_call(
        stack_kernel,
        out_shape=pltpu.VMEM((NX, BPC, parts, width, CB), jnp.bfloat16),
        in_specs=[
            pl.BlockSpec(memory_space=pltpu.SMEM),
            pl.BlockSpec(memory_space=pltpu.SMEM),
            pl.BlockSpec(memory_space=pltpu.HBM),
        ],
        out_specs=pl.BlockSpec(memory_space=pl.ANY),
        scratch_shapes=[
            pltpu.VMEM((windows, parts, band, width), jnp.bfloat16),
            pltpu.VMEM((width // 128, parts * nb * windows, 128), jnp.float32),
            pltpu.VMEM((NX, BPC, parts, 2, windows, 2 * CB), jnp.bfloat16),
            pltpu.VMEM((2, BPC, parts, NZ, 2, 4 * windows, 2 * CB), jnp.bfloat16),
            pltpu.VMEM((BPC, parts, NZ, 4 * windows, 2 * CB), jnp.bfloat16),
            pltpu.VMEM((BPC, 2, 2, parts, width, CB), jnp.bfloat16),
        ] + [pltpu.SemaphoreType.DMA(s) for s in sems],
        compiler_params=pltpu.CompilerParams(
            collective_id=0, has_side_effects=True, vmem_limit_bytes=54 * 2**20
        ),
        cost_estimate=pl.CostEstimate(flops=6_442_450_944, bytes_accessed=16 * 2**20, transcendentals=0),
        name="stack",
    )(kept_bins, keep_mask, spectra)
    return tiles.reshape(nb, parts, width, CB)


def solution(mesh):
    in_specs = (P("col", None, None, "row"), P(), P("col"))
    out_specs = P(None, None, "row", "col")
    return jax.shard_map(
        per_device, mesh=mesh, in_specs=in_specs, out_specs=out_specs, check_vma=False
    )
```

```python
import functools
import math

import jax
import jax.numpy as jnp
from jax import lax
from jax.experimental import pallas as pl
from jax.experimental.pallas import tpu as pltpu
from jax.sharding import PartitionSpec as P

MESH = pl.DeviceIdType.MESH
NX, NY, NZ = 4, 4, 8
BPC = 6
CB = 128
NH = 2


def stack_kernel(
    bins_ref, mask_ref, spectra, out, raw, picked, white, R, C, O,
    in_sem, s1_send, s1_recv, z_send, z_recv, c_send, c_recv, b_send, b_recv, o_send, o_recv,
):
    row, col = lax.axis_index("row"), lax.axis_index("col")
    y, xh = row // 2, row % 2
    xl, z, c = col // 16, (col // 2) % 8, col % 2
    x = xh * 2 + xl
    slot = xl * 2 + c

    def at(x_, y_, z_, c_):
        return ((y_ % NY) * 2 + x_ // 2, (x_ % 2) * 16 + (z_ % NZ) * 2 + c_)

    holder = (z % 4) // 2
    source = (c == holder) & (y % 2 == z // 4)
    to_core = y // 2
    y_from = 2 * c + z // 4

    barrier = pltpu.get_barrier_semaphore()

    def greet(who):
        pl.semaphore_signal(barrier, inc=1, device_id=who, device_id_type=MESH)

    ring = [at((x + dx) % NX, y, z, (c + dc) % 2) for dx in range(NX) for dc in range(2) if dx or dc]
    ring += [at(x, y, z + 1, c), at(x, y, z + NZ - 1, c)]
    for who in ring:
        greet(who)

    @pl.when(y_from != y)
    def _():
        greet(at(x, y_from, z, holder))

    windows, parts, band, width = raw.shape
    nb = bins_ref.shape[0]

    def in_copy(i):
        part = pl.ds(4 * i, 4)
        return pltpu.make_async_copy(spectra.at[part], raw.at[part], in_sem.at[i])

    for i in range(windows // 4):
        in_copy(i).start()
    rows = lax.broadcasted_iota(jnp.int32, (parts * nb, parts * band), 0)
    cols = lax.broadcasted_iota(jnp.int32, (parts * nb, parts * band), 1)
    place = jnp.full((parts * nb, parts * band), -1, jnp.int32)
    for f in range(nb):
        for p in range(parts):
            place = jnp.where(rows == p * nb + f, bins_ref[f] + p * band, place)
    hot = jnp.where(cols == place, 1.0, 0.0).astype(jnp.bfloat16)

    def whiten(i, carry):
        in_copy(i).wait()
        for k in range(4):
            w = 4 * i + k
            block = raw[w].reshape(parts * band, width)
            wide = block.astype(jnp.float32)
            power = jnp.sum(wide * wide, axis=0, keepdims=True) * (1.0 / (parts * band))
            factor = mask_ref[w].astype(jnp.float32) / jnp.sqrt(power + 1e-06)
            kept = jnp.dot(hot, block, preferred_element_type=jnp.float32) * factor
            for l in range(width // 128):
                picked[l, pl.ds(w, parts * nb, stride=windows), :] = kept[:, l * 128:(l + 1) * 128]
        return carry

    lax.fori_loop(0, windows // 4, whiten, 0)
    pl.semaphore_wait(barrier, len(ring) + jnp.where(source, NY - 1, 0))

    def remote(src, dst, ssem, rsem, who):
        return pltpu.make_async_remote_copy(
            src_ref=src, dst_ref=dst, send_sem=ssem, recv_sem=rsem, device_id=who, device_id_type=MESH
        )

    def s1_copy(j, xt):
        return remote(
            white.at[xt, j], R.at[xh, j, :, 0, :, pl.ds(pl.multiple_of(slot * 16, 16), 16), :],
            s1_send.at[xt], s1_recv.at[j, xl], at(xt, y, z, xh),
        )

    def s1_start(j):
        for d in range(NX):
            xt = (x + d) % NX
            self_ = (xt == x) & (xh == c)

            @pl.when(self_)
            def _():
                pltpu.make_async_copy(
                    white.at[xt, j], R.at[xh, j, :, 0, :, pl.ds(pl.multiple_of(slot * 16, 16), 16), :],
                    s1_recv.at[j, xl],
                ).start()

            @pl.when(jnp.logical_not(self_))
            def _():
                s1_copy(j, xt).start()

    def s1_wait(j, h):
        dst = R.at[c, j, :, 0, :, pl.ds(h * 32, 32)]
        pltpu.make_async_copy(dst, dst, s1_recv.at[j, h]).wait()

    def z_copy(j, t, p, h, way):
        rows = pl.ds(h * (64 // NH), 64 // NH)
        if way == 0:
            here, there, who = max(2 * t - 1, 0), 2 * t + 1, at(x, y, z + 1, c)
        else:
            here, there, who = 2 * t, 7 if t == 3 else 2 * t + 2, at(x, y, z + NZ - 1, c)
        return remote(
            R.at[c, j, p, here, :, rows], R.at[c, j, p, there, :, rows],
            z_send.at[way], z_recv.at[j % 2, t, p, h, way], who,
        )

    def z_goes(t, p, way):
        return 0 <= t < 3 or (t == 3 and way == p)

    def span(t):
        return pl.ds(0, 1) if t == 0 else pl.ds(7, 1) if t == 4 else pl.ds(2 * t - 1, 2)

    def b_copy(j, view):
        view = R.at[c, j, :, view]
        return remote(view, view, b_send, b_recv.at[j], at(x, y, z, 1 - c))

    def c_copy(j, view, d):
        src, dst = R.at[c, j, :, view, z % 2], C.at[j, :, view]
        return remote(src, dst, c_send.at[d], c_recv.at[j], at(x, y + d, z, to_core))

    def share(j, t):
        @pl.when(source)
        def _():
            for d in (2, 1, 3):
                c_copy(j, span(t), d).start()

            @pl.when(c == to_core)
            def _():
                pltpu.make_async_copy(
                    R.at[c, j, :, span(t), z % 2], C.at[j, :, span(t)], c_recv.at[j]
                ).start()

            @pl.when(c != to_core)
            def _():
                c_copy(j, span(t), 0).start()

        b_copy(j, span(t)).start()

    def shared(j):
        dst = R.at[1 - c, j]
        pltpu.make_async_copy(dst, dst, b_recv.at[j]).wait()
        pltpu.make_async_copy(C.at[j], C.at[j], c_recv.at[j]).wait()

    def hop(j, t):
        for h in range(NH):
            if t == 0:
                s1_wait(j, h)
            for p in range(parts):
                for way in range(2):
                    if z_goes(t - 1, p, way):
                        z_copy(j, t - 1, p, h, way).wait_recv()
                    if z_goes(t, p, way):
                        z_copy(j, t, p, h, way).start()
        share(j, t)

    scale = 1.0 / math.sqrt(512)
    dims = (((0,), (0,)), ((), ()))

    def product(j, turn, m):
        xr = jnp.where(turn == 0, 1 - x // 2, x // 2)
        depth = R.shape[3] * R.shape[5]
        rows = pl.ds(m * 256, 256)
        r0, r1 = (C[j, p].reshape(depth, 2 * CB) for p in range(parts))
        l0, l1 = (R[xr, j, p, :, m].reshape(depth, 256) for p in range(parts))
        both = jnp.concatenate([r0, r1], 1)
        dot = functools.partial(lax.dot_general, dimension_numbers=dims, preferred_element_type=jnp.float32)
        by0, by1 = dot(l0, both), dot(l1, both)
        re = ((by0[:, :2 * CB] + by1[:, 2 * CB:]) * scale).astype(jnp.bfloat16)
        im = ((by1[:, :2 * CB] - by0[:, 2 * CB:]) * scale).astype(jnp.bfloat16)
        for k in range(2):
            O[j, xr, k, 0, rows, :] = re[:, k * CB:(k + 1) * CB]
            O[j, xr, k, 1, rows, :] = im[:, k * CB:(k + 1) * CB]
        o_start(j, xr, m)

    def o_copy(j, xr, k, m):
        rows = pl.ds(m * 256, 256)
        return remote(
            O.at[j, xr, k, :, rows], out.at[x, j, :, rows],
            o_send.at[xr * 2 + k], o_recv, at(2 * xr + c, y, z, k)
        )

    def is_self(xr, k):
        return (2 * xr + c == x) & (k == c)

    def o_start(j, xr, m):
        rows = pl.ds(m * 256, 256)
        for k in range(2):
            @pl.when(is_self(xr, k))
            def _():
                pltpu.make_async_copy(
                    O.at[j, xr, k, :, rows], out.at[x, j, :, rows], o_recv
                ).start()

            @pl.when(jnp.logical_not(is_self(xr, k)))
            def _():
                o_copy(j, xr, k, m).start()

    def s1_bin(j):
        for l in range(width // 128):
            for xt in range(NX):
                for p in range(parts):
                    start = pl.multiple_of((p * nb + xt * BPC + j) * windows, windows)
                    tile = picked[l, pl.ds(start, windows), :]
                    white[xt, j, p, l // 2, :, l % 2 * 128:(l % 2 + 1) * 128] = tile.astype(jnp.bfloat16)
        s1_start(j)

    s1_bin(0)
    hop(0, 0)
    s1_bin(1)
    s1_bin(2)
    hop(0, 1)
    s1_bin(3)
    s1_bin(4)
    s1_bin(5)
    hop(0, 2)
    hop(1, 0)

    def step(i, carry):
        def on(j, *work):
            @pl.when((j >= 0) & (j < BPC))
            def _():
                for f, *args in work:
                    f(j, *args)

        on(i, (hop, 3))
        on(i - 1, (product, 0, 1))
        on(i + 1, (hop, 1))
        on(i - 1, (product, 1, 0))
        on(i, (hop, 4))
        on(i - 1, (product, 1, 1))
        on(i + 1, (hop, 2))
        on(i + 2, (hop, 0))
        on(i, (shared,), (product, 0, 0))
        return carry

    lax.fori_loop(0, BPC + 1, step, 0)

    def sent(view, sem):
        remote(view, view, sem, o_recv, at(x, y, z, 1 - c)).wait_send()

    for xt in range(NX):
        @pl.when(jnp.logical_not((xt == x) & (xh == c)))
        def _():
            sent(white.at[xt], s1_send.at[xt])
    for way in range(2):
        sent(R.at[c, :, 0, pl.ds(0, 7)], z_send.at[way])
    sent(R.at[c], b_send)

    @pl.when(source)
    def _():
        for d in range(1, 4):
            sent(C, c_send.at[d])

        @pl.when(c != to_core)
        def _():
            sent(C, c_send.at[0])

    for xr in range(2):
        for k in range(2):
            @pl.when(jnp.logical_not(is_self(xr, k)))
            def _():
                sent(O.at[:, xr, k], o_send.at[xr * 2 + k])
    pltpu.make_async_copy(out, out, o_recv).wait()


def per_device(spectra, kept_bins, keep_mask):
    windows, parts, band, width = spectra.shape
    nb = kept_bins.shape[0]
    sems = [(windows // 4,), (NX,), (BPC, NH), (2,), (2, 4, 2, NH, 2), (NY,), (BPC,), (), (BPC,), (4,), ()]
    tiles = pl.pallas_call(
        stack_kernel,
        out_shape=pltpu.VMEM((NX, BPC, parts, width, CB), jnp.bfloat16),
        in_specs=[
            pl.BlockSpec(memory_space=pltpu.SMEM),
            pl.BlockSpec(memory_space=pltpu.SMEM),
            pl.BlockSpec(memory_space=pltpu.HBM),
        ],
        out_specs=pl.BlockSpec(memory_space=pl.ANY),
        scratch_shapes=[
            pltpu.VMEM((windows, parts, band, width), jnp.bfloat16),
            pltpu.VMEM((width // 128, parts * nb * windows, 128), jnp.float32),
            pltpu.VMEM((NX, BPC, parts, 2, windows, 2 * CB), jnp.bfloat16),
            pltpu.VMEM((2, BPC, parts, NZ, 2, 4 * windows, 2 * CB), jnp.bfloat16),
            pltpu.VMEM((BPC, parts, NZ, 4 * windows, 2 * CB), jnp.bfloat16),
            pltpu.VMEM((BPC, 2, 2, parts, width, CB), jnp.bfloat16),
        ] + [pltpu.SemaphoreType.DMA(s) for s in sems],
        compiler_params=pltpu.CompilerParams(
            collective_id=0, has_side_effects=True, vmem_limit_bytes=54 * 2**20
        ),
        cost_estimate=pl.CostEstimate(flops=6_442_450_944, bytes_accessed=16 * 2**20, transcendentals=0),
        name="stack",
    )(kept_bins, keep_mask, spectra)
    return tiles.reshape(nb, parts, width, CB)


def solution(mesh):
    in_specs = (P("col", None, None, "row"), P(), P("col"))
    out_specs = P(None, None, "row", "col")
    return jax.shard_map(
        per_device, mesh=mesh, in_specs=in_specs, out_specs=out_specs, check_vma=False
    )
```

```python
import functools
import math

import jax
import jax.numpy as jnp
from jax import lax
from jax.experimental import pallas as pl
from jax.experimental.pallas import tpu as pltpu
from jax.sharding import PartitionSpec as P

MESH = pl.DeviceIdType.MESH
NX, NY, NZ = 4, 4, 8
BPC = 6
CB = 128
NH = 2


def stack_kernel(
    bins_ref, mask_ref, spectra, out, raw, picked, white, R, C, O,
    in_sem, s1_send, s1_recv, z_send, z_recv, c_send, c_recv, b_send, b_recv, o_send, o_recv,
):
    row, col = lax.axis_index("row"), lax.axis_index("col")
    y, xh = row // 2, row % 2
    xl, z, c = col // 16, (col // 2) % 8, col % 2
    x = xh * 2 + xl
    slot = xl * 2 + c

    def at(x_, y_, z_, c_):
        return ((y_ % NY) * 2 + x_ // 2, (x_ % 2) * 16 + (z_ % NZ) * 2 + c_)

    holder = (z % 4) // 2
    source = (c == holder) & (y % 2 == z // 4)
    to_core = y // 2
    y_from = 2 * c + z // 4

    barrier = pltpu.get_barrier_semaphore()

    def greet(who):
        pl.semaphore_signal(barrier, inc=1, device_id=who, device_id_type=MESH)

    ring = [at((x + dx) % NX, y, z, (c + dc) % 2) for dx in range(NX) for dc in range(2) if dx or dc]
    ring += [at(x, y, z + 1, c), at(x, y, z + NZ - 1, c)]
    for who in ring:
        greet(who)

    @pl.when(y_from != y)
    def _():
        greet(at(x, y_from, z, holder))

    windows, parts, band, width = raw.shape
    nb = bins_ref.shape[0]

    def in_copy(i):
        part = pl.ds(4 * i, 4)
        return pltpu.make_async_copy(spectra.at[part], raw.at[part], in_sem.at[i])

    for i in range(windows // 4):
        in_copy(i).start()
    rows = lax.broadcasted_iota(jnp.int32, (parts * nb, parts * band), 0)
    cols = lax.broadcasted_iota(jnp.int32, (parts * nb, parts * band), 1)
    place = jnp.full((parts * nb, parts * band), -1, jnp.int32)
    for f in range(nb):
        for p in range(parts):
            place = jnp.where(rows == p * nb + f, bins_ref[f] + p * band, place)
    hot = jnp.where(cols == place, 1.0, 0.0).astype(jnp.bfloat16)

    def whiten(i, carry):
        in_copy(i).wait()
        for k in range(4):
            w = 4 * i + k
            block = raw[w].reshape(parts * band, width)
            wide = block.astype(jnp.float32)
            power = jnp.sum(wide * wide, axis=0, keepdims=True) * (1.0 / (parts * band))
            factor = mask_ref[w].astype(jnp.float32) / jnp.sqrt(power + 1e-06)
            kept = jnp.dot(hot, block, preferred_element_type=jnp.float32) * factor
            for l in range(width // 128):
                picked[l, pl.ds(w, parts * nb, stride=windows), :] = kept[:, l * 128:(l + 1) * 128]
        return carry

    lax.fori_loop(0, windows // 4, whiten, 0)
    pl.semaphore_wait(barrier, len(ring) + jnp.where(source, NY - 1, 0))

    def remote(src, dst, ssem, rsem, who):
        return pltpu.make_async_remote_copy(
            src_ref=src, dst_ref=dst, send_sem=ssem, recv_sem=rsem, device_id=who, device_id_type=MESH
        )

    def s1_copy(j, xt):
        return remote(
            white.at[xt, j], R.at[xh, j, :, 0, :, pl.ds(pl.multiple_of(slot * 16, 16), 16), :],
            s1_send.at[xt], s1_recv.at[j, xl], at(xt, y, z, xh),
        )

    def s1_start(j):
        for d in range(NX):
            xt = (x + d) % NX
            self_ = (xt == x) & (xh == c)

            @pl.when(self_)
            def _():
                pltpu.make_async_copy(
                    white.at[xt, j], R.at[xh, j, :, 0, :, pl.ds(pl.multiple_of(slot * 16, 16), 16), :],
                    s1_recv.at[j, xl],
                ).start()

            @pl.when(jnp.logical_not(self_))
            def _():
                s1_copy(j, xt).start()

    def s1_wait(j, h):
        dst = R.at[c, j, :, 0, :, pl.ds(h * 32, 32)]
        pltpu.make_async_copy(dst, dst, s1_recv.at[j, h]).wait()

    def z_copy(j, t, p, h, way):
        rows = pl.ds(h * (64 // NH), 64 // NH)
        if way == 0:
            here, there, who = max(2 * t - 1, 0), 2 * t + 1, at(x, y, z + 1, c)
        else:
            here, there, who = 2 * t, 7 if t == 3 else 2 * t + 2, at(x, y, z + NZ - 1, c)
        return remote(
            R.at[c, j, p, here, :, rows], R.at[c, j, p, there, :, rows],
            z_send.at[way], z_recv.at[j % 2, t, p, h, way], who,
        )

    def z_goes(t, p, way):
        return 0 <= t < 3 or (t == 3 and way == p)

    def span(t):
        return pl.ds(0, 1) if t == 0 else pl.ds(7, 1) if t == 4 else pl.ds(2 * t - 1, 2)

    def b_copy(j, view):
        view = R.at[c, j, :, view]
        return remote(view, view, b_send, b_recv.at[j], at(x, y, z, 1 - c))

    def c_copy(j, view, d):
        src, dst = R.at[c, j, :, view, z % 2], C.at[j, :, view]
        return remote(src, dst, c_send.at[d], c_recv.at[j], at(x, y + d, z, to_core))

    def share(j, t):
        @pl.when(source)
        def _():
            for d in (2, 1, 3):
                c_copy(j, span(t), d).start()

            @pl.when(c == to_core)
            def _():
                pltpu.make_async_copy(
                    R.at[c, j, :, span(t), z % 2], C.at[j, :, span(t)], c_recv.at[j]
                ).start()

            @pl.when(c != to_core)
            def _():
                c_copy(j, span(t), 0).start()

        if t in (2, 4):
            b_copy(j, pl.ds(0, 5) if t == 2 else pl.ds(5, 3)).start()

    def shared(j):
        dst = R.at[1 - c, j]
        pltpu.make_async_copy(dst, dst, b_recv.at[j]).wait()
        pltpu.make_async_copy(C.at[j], C.at[j], c_recv.at[j]).wait()

    def hop(j, t):
        for h in range(NH):
            if t == 0:
                s1_wait(j, h)
            for p in range(parts):
                for way in range(2):
                    if z_goes(t - 1, p, way):
                        z_copy(j, t - 1, p, h, way).wait_recv()
                    if z_goes(t, p, way):
                        z_copy(j, t, p, h, way).start()
        share(j, t)

    scale = 1.0 / math.sqrt(512)
    dims = (((0,), (0,)), ((), ()))

    def product(j, turn, m):
        xr = jnp.where(turn == 0, 1 - x // 2, x // 2)
        depth = R.shape[3] * R.shape[5]
        rows = pl.ds(m * 256, 256)
        r0, r1 = (C[j, p].reshape(depth, 2 * CB) for p in range(parts))
        l0, l1 = (R[xr, j, p, :, m].reshape(depth, 256) for p in range(parts))
        both = jnp.concatenate([r0, r1], 1)
        dot = functools.partial(lax.dot_general, dimension_numbers=dims, preferred_element_type=jnp.float32)
        by0, by1 = dot(l0, both), dot(l1, both)
        re = ((by0[:, :2 * CB] + by1[:, 2 * CB:]) * scale).astype(jnp.bfloat16)
        im = ((by1[:, :2 * CB] - by0[:, 2 * CB:]) * scale).astype(jnp.bfloat16)
        for k in range(2):
            O[j, xr, k, 0, rows, :] = re[:, k * CB:(k + 1) * CB]
            O[j, xr, k, 1, rows, :] = im[:, k * CB:(k + 1) * CB]
        o_start(j, xr, m)

    def o_copy(j, xr, k, m):
        rows = pl.ds(m * 256, 256)
        return remote(
            O.at[j, xr, k, :, rows], out.at[x, j, :, rows],
            o_send.at[xr * 2 + k], o_recv, at(2 * xr + c, y, z, k)
        )

    def is_self(xr, k):
        return (2 * xr + c == x) & (k == c)

    def o_start(j, xr, m):
        rows = pl.ds(m * 256, 256)
        for k in range(2):
            @pl.when(is_self(xr, k))
            def _():
                pltpu.make_async_copy(
                    O.at[j, xr, k, :, rows], out.at[x, j, :, rows], o_recv
                ).start()

            @pl.when(jnp.logical_not(is_self(xr, k)))
            def _():
                o_copy(j, xr, k, m).start()

    def s1_bin(j):
        for l in range(width // 128):
            for xt in range(NX):
                for p in range(parts):
                    start = pl.multiple_of((p * nb + xt * BPC + j) * windows, windows)
                    tile = picked[l, pl.ds(start, windows), :]
                    white[xt, j, p, l // 2, :, l % 2 * 128:(l % 2 + 1) * 128] = tile.astype(jnp.bfloat16)
        s1_start(j)

    s1_bin(0)
    hop(0, 0)
    s1_bin(1)
    s1_bin(2)
    hop(0, 1)
    s1_bin(3)
    s1_bin(4)
    s1_bin(5)
    hop(0, 2)
    hop(1, 0)

    def step(i, carry):
        def on(j, *work):
            @pl.when((j >= 0) & (j < BPC))
            def _():
                for f, *args in work:
                    f(j, *args)

        on(i, (hop, 3))
        on(i - 1, (product, 0, 1), (product, 1, 0))
        on(i + 1, (hop, 1))
        on(i - 1, (product, 1, 1))
        on(i, (hop, 4))
        on(i + 1, (hop, 2))
        on(i + 2, (hop, 0))
        on(i, (shared,), (product, 0, 0))
        return carry

    lax.fori_loop(0, BPC + 1, step, 0)

    def sent(view, sem):
        remote(view, view, sem, o_recv, at(x, y, z, 1 - c)).wait_send()

    for xt in range(NX):
        @pl.when(jnp.logical_not((xt == x) & (xh == c)))
        def _():
            sent(white.at[xt], s1_send.at[xt])
    for way in range(2):
        sent(R.at[c, :, 0, pl.ds(0, 7)], z_send.at[way])
    sent(R.at[c], b_send)

    @pl.when(source)
    def _():
        for d in range(1, 4):
            sent(C, c_send.at[d])

        @pl.when(c != to_core)
        def _():
            sent(C, c_send.at[0])

    for xr in range(2):
        for k in range(2):
            @pl.when(jnp.logical_not(is_self(xr, k)))
            def _():
                sent(O.at[:, xr, k], o_send.at[xr * 2 + k])
    pltpu.make_async_copy(out, out, o_recv).wait()


def per_device(spectra, kept_bins, keep_mask):
    windows, parts, band, width = spectra.shape
    nb = kept_bins.shape[0]
    sems = [(windows // 4,), (NX,), (BPC, NH), (2,), (2, 4, 2, NH, 2), (NY,), (BPC,), (), (BPC,), (4,), ()]
    tiles = pl.pallas_call(
        stack_kernel,
        out_shape=pltpu.VMEM((NX, BPC, parts, width, CB), jnp.bfloat16),
        in_specs=[
            pl.BlockSpec(memory_space=pltpu.SMEM),
            pl.BlockSpec(memory_space=pltpu.SMEM),
            pl.BlockSpec(memory_space=pltpu.HBM),
        ],
        out_specs=pl.BlockSpec(memory_space=pl.ANY),
        scratch_shapes=[
            pltpu.VMEM((windows, parts, band, width), jnp.bfloat16),
            pltpu.VMEM((width // 128, parts * nb * windows, 128), jnp.float32),
            pltpu.VMEM((NX, BPC, parts, 2, windows, 2 * CB), jnp.bfloat16),
            pltpu.VMEM((2, BPC, parts, NZ, 2, 4 * windows, 2 * CB), jnp.bfloat16),
            pltpu.VMEM((BPC, parts, NZ, 4 * windows, 2 * CB), jnp.bfloat16),
            pltpu.VMEM((BPC, 2, 2, parts, width, CB), jnp.bfloat16),
        ] + [pltpu.SemaphoreType.DMA(s) for s in sems],
        compiler_params=pltpu.CompilerParams(
            collective_id=0, has_side_effects=True, vmem_limit_bytes=54 * 2**20
        ),
        cost_estimate=pl.CostEstimate(flops=6_442_450_944, bytes_accessed=16 * 2**20, transcendentals=0),
        name="stack",
    )(kept_bins, keep_mask, spectra)
    return tiles.reshape(nb, parts, width, CB)


def solution(mesh):
    in_specs = (P("col", None, None, "row"), P(), P("col"))
    out_specs = P(None, None, "row", "col")
    return jax.shard_map(
        per_device, mesh=mesh, in_specs=in_specs, out_specs=out_specs, check_vma=False
    )
```
